128 devices in a mesh: dp: 4 (over x_hi, core), tensor: 32 (over z, y, x_lo).
Axes of the slice: x: 4 (x_hi: 2, x_lo: 2; x = x_hi * 2 + x_lo), y: 4, z: 4, core: 2. Of those that a mesh axis runs over, the one named last changes fastest.
Arguments:
- grad_act: bfloat16 [8192, 8192], P(('dp', 'tensor')), parts along dimension 0, may hold values from -6 to 6
- x_pre: bfloat16 [8192, 8192], P(('dp', 'tensor')), parts along dimension 0, may hold values from -6 to 6
- grad_gate: bfloat16 [8192, 8192], P('dp', 'tensor'), parts along dimension 0, may hold values from -6 to 6
- normed_input: bfloat16 [8192, 4096], P('dp'), parts along dimension 0, may hold values from -0.125 to 0.125
- conv_weight: float32 [4, 8192], P(None, 'tensor'), may hold values from -3 to 3
- conv_bias: float32 [8192], P('tensor'), may hold values from -1 to 1
- up_x: bfloat16 [4096, 8192], P(None, 'tensor'), may hold values from -0.09375 to 0.09375
- up_z: bfloat16 [4096, 8192], P(None, 'tensor'), may hold values from -0.09375 to 0.09375
Outputs:
- grad_input: bfloat16 [8192, 4096], P(('dp', 'tensor')), parts along dimension 0
- grad_up_x: float32 [16384, 8192], P('dp', 'tensor'), parts along dimension 0
- grad_up_z: float32 [16384, 8192], P('dp', 'tensor'), parts along dimension 0
- grad_conv_weight: float32 [16, 8192], P('dp', 'tensor'), parts along dimension 0
- grad_conv_bias: float32 [32768], P(('dp', 'tensor')), parts along dimension 0
The draws below stay inside these ranges and needn't reach their ends.
There are 4 independent parts, one for each index of `dp`. The reference program is written for one: setup_inputs(seed, part) draws one part's arguments, and reference() takes and returns one part's arrays. A program takes and returns all parts, laid end to end along the dimension named above; an argument that names none is the same for every part. Nothing has to cross between parts.
All inputs are finite; a program needn't handle non-finite values.
Results may differ from the reference program's by a relative error of at most 0.0065.
Values may be sent and summed in bfloat16 or wider, within the bound.
A program may use at most 192 MiB of HBM per device.

```python
import jax
import jax.numpy as jnp

D = 4096
INNER = 8192
KERNEL = 4
TOKENS = 2048


def block_scale(key, extent, split, least, top_value):
    level = 1.0
    for position, blocks in split:
        steps = jax.random.uniform(jax.random.fold_in(jax.random.fold_in(key, 6), position), (blocks,), jnp.float32, least / len(split), top_value / len(split))
        level = level * jnp.repeat(jnp.exp(steps), extent[position] // blocks).reshape((-1,) + (1,) * (len(extent) - 1 - position))
    return level


def scatter_about(stream_key, dims, spread, reach, split=(), kind=jnp.bfloat16):
    array = jax.random.normal(stream_key, dims, jnp.float32) * spread
    if len(split) > 0:
        array = block_scale(stream_key, dims, split, -0.22, 0.18) * array
    return jnp.clip(array, min=-reach, max=reach).astype(kind)


def setup_inputs(seed: int = 0, part: int = 0) -> dict:
    arg_keys = jax.random.split(jax.random.key(seed), 9)
    part_keys = jax.random.split(jax.random.fold_in(arg_keys[8], part), 9)
    return {
        "grad_act": scatter_about(part_keys[0], (TOKENS, INNER), 1.0, 6.0, ((0, 32),)),
        "x_pre": scatter_about(part_keys[1], (TOKENS, INNER), 1.0, 6.0, ((0, 32),)),
        "grad_gate": scatter_about(part_keys[2], (TOKENS, INNER), 1.0, 6.0, ((1, 32),)),
        "normed_input": scatter_about(part_keys[3], (TOKENS, D), TOKENS ** -0.5, 0.125),
        "conv_weight": scatter_about(arg_keys[4], (KERNEL, INNER), 0.5, 3.0, ((1, 32),), jnp.float32),
        "conv_bias": jnp.clip(jax.random.uniform(arg_keys[5], (INNER,), jnp.float32, -1.0, 1.0) * block_scale(arg_keys[5], (INNER,), ((0, 32),), -0.4, 0.0), -1.0, 1.0),
        "up_x": scatter_about(arg_keys[6], (D, INNER), D ** -0.5, 0.09375, ((1, 32),)),
        "up_z": scatter_about(arg_keys[7], (D, INNER), D ** -0.5, 0.09375, ((1, 32),)),
    }


def reference(grad_act, x_pre, grad_gate, normed_input, conv_weight, conv_bias, up_x, up_z):
    token_count = x_pre.shape[0]
    inputs_pad = jnp.concatenate([jnp.zeros((KERNEL - 1, INNER), jnp.float32), x_pre.astype(jnp.float32)], axis=0)
    conv_value = conv_bias[None, :] + sum(conv_weight[offset][None, :] * inputs_pad[KERNEL - 1 - offset:KERNEL - 1 - offset + token_count] for offset in range(KERNEL))
    gate_sig = jax.nn.sigmoid(conv_value)
    cell_grad = (grad_act.astype(jnp.float32) * gate_sig * (1.0 + conv_value * (1.0 - gate_sig))).astype(jnp.bfloat16)
    cell_float = cell_grad.astype(jnp.float32)
    cell_pad = jnp.concatenate([cell_float, jnp.zeros((KERNEL - 1, INNER), jnp.float32)], axis=0)
    grad_x = sum(conv_weight[offset][None, :] * cell_pad[offset:offset + token_count] for offset in range(KERNEL)).astype(jnp.bfloat16)
    weight_grad = jnp.stack([jnp.sum(inputs_pad[KERNEL - 1 - offset:KERNEL - 1 - offset + token_count] * cell_float, axis=0) for offset in range(KERNEL)])
    bias_grad = jnp.sum(cell_float, axis=0)
    grad_up_x = jnp.dot(normed_input.T, grad_x, preferred_element_type=jnp.float32)
    grad_up_z = jnp.dot(normed_input.T, grad_gate, preferred_element_type=jnp.float32)
    summed = jnp.dot(grad_x, up_x.T, preferred_element_type=jnp.float32) + jnp.dot(grad_gate, up_z.T, preferred_element_type=jnp.float32)
    return summed.astype(jnp.bfloat16), grad_up_x, grad_up_z, weight_grad, bias_grad
```

```python
import jax
import jax.numpy as jnp
from jax import lax
from jax.experimental import pallas as pl
from jax.experimental.pallas import tpu as pltpu
from jax.sharding import PartitionSpec as P

MESH = pl.DeviceIdType.MESH
F32 = jnp.float32
BF16 = jnp.bfloat16
TAPS = 4
GROUP = 32
ROWS = 64
WIDTH = 256
DIM = 4096
TOKENS = GROUP * ROWS
CHUNKS = 4
CHUNK = DIM // CHUNKS
TILE = CHUNK // 4


def kernel(
    act_hbm,
    pre_hbm,
    gate_hbm,
    normed_hbm,
    taps_ref,
    bias_ref,
    upx_hbm,
    upz_hbm,
    out_ref,
    gux_hbm,
    guz_hbm,
    small_ref,
    act_buf,
    pre_buf,
    gate_buf,
    gate_t,
    gx_buf,
    gx_t,
    left,
    right,
    normed,
    stage,
    send1,
    recv1,
    send2,
    recv2,
    total,
    load_sem,
    a2a_send,
    a2a_recv,
    w_send,
    w_recv,
    fwd_send,
    fwd_recv,
    pair_send,
    pair_recv,
    stage_sem,
    s1_send,
    s1_recv,
    s2_send,
    s2_recv,
):
    dp = lax.axis_index("dp")
    me = lax.axis_index("tensor")
    z, y, x = me // 8, (me // 2) % 4, me % 2
    core = dp % 2
    partner = (dp, me + 1 - 2 * x)
    outside = ((dp + 2) % 4, me + 1 - 2 * x)
    sibling = (dp + 1 - 2 * core, me)

    def group_peer(step):
        return (me + step) % GROUP

    def local(src, dst, sem):
        return pltpu.make_async_copy(src, dst, sem)

    loads = [
        local(gate_hbm, gate_buf, load_sem.at[0]),
        local(normed_hbm, normed, load_sem.at[1]),
        local(gate_hbm.at[:, x], left.at[:, :, pl.ds(2 * WIDTH, WIDTH)], load_sem.at[2]),
        local(upx_hbm, right.at[:, pl.ds(0, WIDTH)], load_sem.at[3]),
        local(upz_hbm, right.at[:, pl.ds(2 * WIDTH, WIDTH)], load_sem.at[4]),
        local(
            act_hbm.at[:, pl.ds(pl.multiple_of(me * WIDTH, WIDTH), WIDTH)],
            act_buf.at[pl.ds(pl.multiple_of(me * ROWS, ROWS), ROWS)],
            load_sem.at[5],
        ),
        local(
            pre_hbm.at[:, pl.ds(pl.multiple_of(me * WIDTH, WIDTH), WIDTH)],
            pre_buf.at[pl.ds(pl.multiple_of(me * ROWS + 16, 16), ROWS)],
            load_sem.at[6],
        ),
    ]
    for copy in loads:
        copy.start()

    barrier = pltpu.get_barrier_semaphore()

    def greet(step, _):
        pl.semaphore_signal(
            barrier, inc=1, device_id=(dp, group_peer(step)), device_id_type=MESH
        )
        return 0

    lax.fori_loop(1, GROUP, greet, 0)
    pl.semaphore_signal(barrier, inc=1, device_id=outside, device_id_type=MESH)
    pl.semaphore_signal(barrier, inc=1, device_id=sibling, device_id_type=MESH)
    pl.semaphore_wait(barrier, GROUP + 1)

    def remote(src, dst, send, recv, device):
        return pltpu.make_async_remote_copy(
            src_ref=src,
            dst_ref=dst,
            send_sem=send,
            recv_sem=recv,
            device_id=device,
            device_id_type=MESH,
        )

    def weight_rows(q, half):
        return pl.ds(pl.multiple_of(q * CHUNK + half * (CHUNK // 2), CHUNK // 2), CHUNK // 2)

    def weight_copies(q):
        rows = weight_rows(q, core)
        return [
            remote(
                src.at[rows],
                right.at[rows, pl.ds(slot * WIDTH, WIDTH)],
                w_send.at[q, k],
                w_recv.at[q, k],
                outside,
            )
            for k, (src, slot) in enumerate(((upx_hbm, 1), (upz_hbm, 3)))
        ]

    def forward_copies(q):
        rows = weight_rows(q, core)
        return [
            remote(
                right.at[rows, pl.ds(slot * WIDTH, WIDTH)],
                right.at[rows, pl.ds(slot * WIDTH, WIDTH)],
                fwd_send.at[q, k],
                fwd_recv.at[q, k],
                sibling,
            )
            for k, slot in enumerate((1, 3))
        ]

    for copy in weight_copies(0):
        copy.start()

    def exchange(step, _):
        peer = group_peer(step)
        columns = pl.ds(pl.multiple_of(peer * WIDTH, WIDTH), WIDTH)
        remote(
            pre_hbm.at[:, columns],
            pre_buf.at[pl.ds(pl.multiple_of(me * ROWS + 16, 16), ROWS)],
            a2a_send.at[0],
            a2a_recv.at[0],
            (dp, peer),
        ).start()
        remote(
            act_hbm.at[:, columns],
            act_buf.at[pl.ds(pl.multiple_of(me * ROWS, ROWS), ROWS)],
            a2a_send.at[1],
            a2a_recv.at[1],
            (dp, peer),
        ).start()
        return 0

    lax.fori_loop(1, GROUP, exchange, 0)
    gate_pair = remote(
        gate_hbm.at[:, 1 - x],
        left.at[:, :, pl.ds(3 * WIDTH, WIDTH)],
        pair_send.at[0],
        pair_recv.at[0],
        partner,
    )
    gate_pair.start()
    for q in range(1, CHUNKS):
        for copy in weight_copies(q):
            copy.start()

    pre_buf[pl.ds(0, 16), :] = jnp.zeros((16, WIDTH), BF16)
    pre_buf[pl.ds(TOKENS + 16, 16), :] = jnp.zeros((16, WIDTH), BF16)
    act_buf[pl.ds(TOKENS, 16), :] = jnp.zeros((16, WIDTH), BF16)

    def up_gradient(n, slot, turned, result):
        columns = pl.ds(pl.multiple_of(n * 512, 512), 512)
        product = jnp.dot(turned[...], normed[:, columns], preferred_element_type=F32)
        stage[slot] = product.T
        local(stage.at[slot], result.at[columns], stage_sem.at[slot]).start()

    def stage_wait(slot):
        local(stage.at[slot], guz_hbm.at[pl.ds(0, 512)], stage_sem.at[slot]).wait()

    loads[0].wait()

    def turn_gate(b, _):
        pair = jnp.concatenate([gate_buf[b, 0], gate_buf[b, 1]], axis=0).astype(F32)
        gate_t[:, pl.ds(pl.multiple_of(b * 128, 128), 128)] = pair.T.astype(BF16)
        return 0

    lax.fori_loop(0, 16, turn_gate, 0)
    loads[1].wait()

    def gate_step(n, _):
        for slot in range(2):

            @pl.when(n > 0)
            def _():
                stage_wait(slot)

            up_gradient(2 * n + slot, slot, gate_t, guz_hbm)
        return 0

    lax.fori_loop(0, 4, gate_step, 0)

    def forward(q):
        for copy in weight_copies(q):
            copy.wait_recv()
        for copy in forward_copies(q):
            copy.start()

    forward(0)

    loads[5].wait()
    loads[6].wait()
    others = pl.ds(0, TOKENS - ROWS)
    local(pre_buf.at[others], pre_buf.at[others], a2a_recv.at[0]).wait()
    local(act_buf.at[others], act_buf.at[others], a2a_recv.at[1]).wait()

    def convolve(b, sums):
        sums = list(sums)
        for part in range(2):
            lanes = pl.ds(part * 128, 128)
            weights = [taps_ref[pl.ds(j, 1), lanes] for j in range(TAPS)]
            bias = bias_ref[:, lanes]
            halves = []
            for parity in range(2):
                row = pl.multiple_of(b * 128 + parity * ROWS, ROWS)
                window = pre_buf[pl.ds(row, 96), lanes].astype(F32)[8:88]
                incoming = act_buf[pl.ds(row, 80), lanes].astype(F32)[:72]
                shifted = [window[8:]] + [pltpu.roll(window, j, 0)[8:] for j in range(1, TAPS)]
                conv = bias + (
                    weights[0] * shifted[0]
                    + weights[1] * shifted[1]
                    + weights[2] * shifted[2]
                    + weights[3] * shifted[3]
                )
                sig = 1.0 / (1.0 + jnp.exp(-conv))
                cell = (incoming * sig * (1.0 + conv * (1.0 - sig))).astype(BF16).astype(F32)
                grad = weights[0] * cell[:ROWS]
                for j in range(1, TAPS):
                    grad += weights[j] * pltpu.roll(cell, 72 - j, 0)[:ROWS]
                grad = grad.astype(BF16)
                gx_buf[parity, b, :, lanes] = grad
                halves.append(grad.astype(F32))
                inner = cell[:ROWS]
                for j in range(TAPS):
                    k = part * 5 + j
                    sums[k] += (shifted[j][:ROWS] * inner).reshape(8, 8, 128).sum(0)
                sums[part * 5 + 4] += inner.reshape(8, 8, 128).sum(0)
            left[b, :, lanes] = jnp.where(x == 0, halves[0], halves[1]).astype(BF16)
        remote(
            gx_buf.at[1 - x, b],
            left.at[b, :, pl.ds(WIDTH, WIDTH)],
            pair_send.at[1],
            pair_recv.at[1],
            partner,
        ).start()
        return tuple(sums)

    zero = jnp.zeros((8, 128), F32)
    sums = lax.fori_loop(0, 16, convolve, (zero,) * 10)
    for part in range(2):
        rows = [sums[part * 5 + j].sum(0, keepdims=True) for j in range(5)]
        rows.append(jnp.zeros((3, 128), F32))
        small_ref[:, pl.ds(part * 128, 128)] = jnp.concatenate(rows, axis=0)

    def turn_gx(b, _):
        pair = jnp.concatenate([gx_buf[0, b], gx_buf[1, b]], axis=0).astype(F32)
        gx_t[:, pl.ds(pl.multiple_of(b * 128, 128), 128)] = pair.T.astype(BF16)
        return 0

    lax.fori_loop(0, 16, turn_gx, 0)

    def place(s, first):
        along_z = (1 - s) if first else s
        return along_z * z + (1 - along_z) * y

    def neighbour(s, first, step):
        along_z = (1 - s) if first else s
        far_z = (z + step * along_z) % 4
        far_y = (y + step * (1 - along_z)) % 4
        return (dp, (far_z * 4 + far_y) * 2 + x)

    def term(q, s, step, half):
        target = (place(s, True) + step) % 4
        base = target * (4 - 3 * s)
        stride = 1 + 3 * s
        rows = jnp.concatenate([left[base + stride * j] for j in range(4)], axis=0)
        columns = pl.ds(
            pl.multiple_of(q * CHUNK + s * (CHUNK // 2) + half * TILE, TILE), TILE
        )
        return lax.dot_general(
            rows, right[columns, :], (((1,), (1,)), ((), ())), preferred_element_type=F32
        )

    def hop1(q, s, k):
        step = 1 + 2 * (k % 2)
        return remote(
            send1.at[q, s, k],
            recv1.at[q, s, k],
            s1_send,
            s1_recv.at[q, s, k],
            neighbour(s, True, step),
        )

    def hop2(q, s, k):
        step = 1 + 2 * (k % 2)
        return remote(
            send2.at[q, s, k],
            recv2.at[q, s, k],
            s2_send,
            s2_recv.at[q, s, k],
            neighbour(s, False, step),
        )

    def first_terms(q):
        if q > 0:
            forward(q)
        for copy in forward_copies(q):
            copy.wait_recv()

        def body(i, _):
            k, s = i // 2, i % 2
            near = k // 2
            step = 2 - near + 2 * near * (k % 2)
            half = (k + near) % 2
            send1[q, s, k] = term(q, s, step, half).astype(BF16)
            hop1(q, s, k).start()
            return 0

        lax.fori_loop(0, 8, body, 0)

    def passed_terms(q):
        def body(i, _):
            half, s = i // 2, i % 2
            value = term(q, s, 1 + 2 * half, half)
            hop1(q, s, half).wait_recv()
            send1[q, s, 4 + half] = (value + recv1[q, s, half].astype(F32)).astype(BF16)
            hop1(q, s, 4 + half).start()
            return 0

        lax.fori_loop(0, 4, body, 0)

    def own_terms(q):
        def body(i, _):
            half, s = i // 2, i % 2
            value = term(q, s, 0, half)
            hop1(q, s, 4 - 2 * half).wait_recv()
            hop1(q, s, 3 + 2 * half).wait_recv()
            value += recv1[q, s, 4 - 2 * half].astype(F32)
            value += recv1[q, s, 3 + 2 * half].astype(F32)
            total[q, s, half] = value.reshape(4, ROWS, TILE)
            return 0

        lax.fori_loop(0, 4, body, 0)

        def spread(i, _):
            k, s = i // 2, i % 2
            near = k // 2
            step = 2 - near + 2 * near * (k % 2)
            half = (k + near) % 2
            send2[q, s, k] = total[q, s, half, (place(s, False) + step) % 4].astype(BF16)
            hop2(q, s, k).start()
            return 0

        lax.fori_loop(0, 8, spread, 0)

    def passed_rows(q):
        def body(i, _):
            half, s = i // 2, i % 2
            value = total[q, s, half, (place(s, False) + 1 + 2 * half) % 4]
            hop2(q, s, half).wait_recv()
            send2[q, s, 4 + half] = (value + recv2[q, s, half].astype(F32)).astype(BF16)
            hop2(q, s, 4 + half).start()
            return 0

        lax.fori_loop(0, 4, body, 0)

    def finish(q):
        for s in range(2):
            for half in range(2):
                value = total[q, s, half, place(s, False)]
                hop2(q, s, 4 - 2 * half).wait_recv()
                hop2(q, s, 3 + 2 * half).wait_recv()
                value += recv2[q, s, 4 - 2 * half].astype(F32)
                value += recv2[q, s, 3 + 2 * half].astype(F32)
                out_ref[:, pl.ds(q * CHUNK + s * (CHUNK // 2) + half * TILE, TILE)] = (
                    value.astype(BF16)
                )

    def gx_step(n):
        for slot in range(2):
            stage_wait(slot)
            up_gradient(2 * n + slot, slot, gx_t, gux_hbm)

    for i in (2, 3, 4):
        loads[i].wait()
    gate_pair.wait_recv()
    own_part = left.at[:, :, pl.ds(WIDTH, WIDTH)]
    local(own_part, own_part, pair_recv.at[1]).wait()

    first_terms(0)
    first_terms(1)
    passed_terms(0)
    first_terms(2)
    passed_terms(1)
    gx_step(0)
    own_terms(0)
    first_terms(3)
    passed_terms(2)
    gx_step(1)
    own_terms(1)
    passed_rows(0)
    passed_terms(3)
    gx_step(2)
    own_terms(2)
    passed_rows(1)
    finish(0)
    gx_step(3)
    own_terms(3)
    passed_rows(2)
    finish(1)
    passed_rows(3)
    finish(2)
    finish(3)

    for k in range(2):
        local(pre_buf.at[others], pre_buf.at[others], a2a_send.at[k]).wait()
    gate_pair.wait_send()
    local(gx_buf.at[0], gx_buf.at[0], pair_send.at[1]).wait()
    for q in range(CHUNKS):
        for copy in weight_copies(q) + forward_copies(q):
            copy.wait_send()
    local(send1, send1, s1_send).wait()
    local(send2, send2, s2_send).wait()
    for slot in range(2):
        stage_wait(slot)


def per_device(grad_act, x_pre, grad_gate, normed_input, conv_weight, conv_bias, up_x, up_z):
    anywhere = pl.BlockSpec(memory_space=pl.ANY)
    vmem = pl.BlockSpec(memory_space=pltpu.VMEM)
    dma = pltpu.SemaphoreType.DMA
    out, gux, guz, small = pl.pallas_call(
        kernel,
        out_shape=(
            jax.ShapeDtypeStruct((ROWS, DIM), BF16),
            jax.ShapeDtypeStruct((DIM, WIDTH), F32),
            jax.ShapeDtypeStruct((DIM, WIDTH), F32),
            jax.ShapeDtypeStruct((8, WIDTH), F32),
        ),
        in_specs=[anywhere] * 4 + [vmem] * 2 + [anywhere] * 2,
        out_specs=(vmem, anywhere, anywhere, vmem),
        scratch_shapes=[
            pltpu.VMEM((TOKENS + 16, WIDTH), BF16),
            pltpu.VMEM((TOKENS + 32, WIDTH), BF16),
            pltpu.VMEM((16, 2, ROWS, WIDTH), BF16),
            pltpu.VMEM((WIDTH, TOKENS), BF16),
            pltpu.VMEM((2, 16, ROWS, WIDTH), BF16),
            pltpu.VMEM((WIDTH, TOKENS), BF16),
            pltpu.VMEM((16, ROWS, 4 * WIDTH), BF16),
            pltpu.VMEM((DIM, 4 * WIDTH), BF16),
            pltpu.VMEM((TOKENS, DIM), BF16),
            pltpu.VMEM((2, 512, WIDTH), F32),
            pltpu.VMEM((CHUNKS, 2, 6, 256, TILE), BF16),
            pltpu.VMEM((CHUNKS, 2, 6, 256, TILE), BF16),
            pltpu.VMEM((CHUNKS, 2, 6, ROWS, TILE), BF16),
            pltpu.VMEM((CHUNKS, 2, 6, ROWS, TILE), BF16),
            pltpu.VMEM((CHUNKS, 2, 2, 4, ROWS, TILE), F32),
            dma((7,)),
            dma((2,)),
            dma((2,)),
            dma((CHUNKS, 2)),
            dma((CHUNKS, 2)),
            dma((CHUNKS, 2)),
            dma((CHUNKS, 2)),
            dma((2,)),
            dma((2,)),
            dma((2,)),
            dma,
            dma((CHUNKS, 2, 6)),
            dma,
            dma((CHUNKS, 2, 6)),
        ],
        compiler_params=pltpu.CompilerParams(
            collective_id=0, has_side_effects=True, vmem_limit_bytes=62 * 1024 * 1024
        ),
        name="conv_up_backward",
    )(
        grad_act,
        x_pre,
        grad_gate.reshape(16, 2, ROWS, WIDTH),
        normed_input,
        conv_weight,
        conv_bias.reshape(1, WIDTH),
        up_x,
        up_z,
    )
    return out, gux, guz, small[:TAPS], small[TAPS]


def solution(mesh):
    placed = (
        P(("dp", "tensor"), None),
        P(("dp", "tensor"), None),
        P("dp", "tensor"),
        P("dp", None),
        P(None, "tensor"),
        P("tensor"),
        P(None, "tensor"),
        P(None, "tensor"),
    )
    return jax.shard_map(
        per_device,
        mesh=mesh,
        in_specs=placed,
        out_specs=(
            P(("dp", "tensor"), None),
            P("dp", "tensor"),
            P("dp", "tensor"),
            P("dp", "tensor"),
            P(("dp", "tensor")),
        ),
        check_vma=False,
    )
```

```python
import jax
import jax.numpy as jnp
from jax import lax
from jax.experimental import pallas as pl
from jax.experimental.pallas import tpu as pltpu
from jax.sharding import PartitionSpec as P

MESH = pl.DeviceIdType.MESH
F32 = jnp.float32
BF16 = jnp.bfloat16
TAPS = 4
GROUP = 32
ROWS = 64
WIDTH = 256
DIM = 4096
INNER = 8192
HALF = INNER // 2
TOKENS = GROUP * ROWS
CHUNKS = 4
CHUNK = DIM // CHUNKS
TILE = CHUNK // 4


def kernel(
    act_hbm,
    pre_hbm,
    gate_hbm,
    normed_hbm,
    taps_ref,
    bias_ref,
    upx_hbm,
    upz_hbm,
    out_ref,
    gux_hbm,
    guz_hbm,
    small_ref,
    act_buf,
    pre_buf,
    tail_out,
    tail_in,
    head_out,
    head_in,
    params,
    sums_out,
    sums_in,
    gate_far,
    gate_t,
    gx_out,
    gx_far,
    gx_t,
    left,
    right,
    normed,
    stage,
    send1,
    recv1,
    send2,
    recv2,
    total,
    load_sem,
    param_send,
    param_recv,
    halo_send,
    halo_recv,
    gx_send,
    gx_recv,
    sums_send,
    sums_recv,
    w_send,
    w_recv,
    fwd_send,
    fwd_recv,
    pair_send,
    pair_recv,
    stage_sem,
    s1_send,
    s1_recv,
    s2_send,
    s2_recv,
):
    dp = lax.axis_index("dp")
    me = lax.axis_index("tensor")
    z, y, x = me // 8, (me // 2) % 4, me % 2
    spot = me // 2
    core = dp % 2
    partner = (dp, me + 1 - 2 * x)
    outside = ((dp + 2) % 4, me + 1 - 2 * x)
    sibling = (dp + 1 - 2 * core, me)

    def group_peer(step):
        return (me + step) % GROUP

    def local(src, dst, sem):
        return pltpu.make_async_copy(src, dst, sem)

    def remote(src, dst, send, recv, device):
        return pltpu.make_async_remote_copy(
            src_ref=src,
            dst_ref=dst,
            send_sem=send,
            recv_sem=recv,
            device_id=device,
            device_id_type=MESH,
        )

    loads = [
        local(pre_hbm, pre_buf, load_sem.at[0]),
        local(act_hbm, act_buf, load_sem.at[1]),
        local(gate_hbm.at[:, x], left.at[:, :, pl.ds(2 * WIDTH, WIDTH)], load_sem.at[2]),
        local(gate_hbm.at[:, 1 - x], gate_far, load_sem.at[3]),
        local(normed_hbm.at[:, x], normed.at[:, 0], load_sem.at[4]),
        local(normed_hbm.at[:, 1 - x], normed.at[:, 1], load_sem.at[5]),
        local(upx_hbm, right.at[:, pl.ds(0, WIDTH)], load_sem.at[6]),
        local(upz_hbm, right.at[:, pl.ds(2 * WIDTH, WIDTH)], load_sem.at[7]),
    ]
    for copy in loads:
        copy.start()

    barrier = pltpu.get_barrier_semaphore()

    def greet(step, _):
        pl.semaphore_signal(
            barrier, inc=1, device_id=(dp, group_peer(step)), device_id_type=MESH
        )
        return 0

    lax.fori_loop(1, GROUP, greet, 0)
    pl.semaphore_signal(barrier, inc=1, device_id=outside, device_id_type=MESH)
    pl.semaphore_signal(barrier, inc=1, device_id=sibling, device_id_type=MESH)

    loads[0].wait()
    loads[1].wait()
    top = lax.broadcasted_iota(jnp.int32, (8, 1024), 0) < 4
    for part in range(4):
        low = pl.ds(part * 1024, 1024)
        high = pl.ds(HALF + part * 1024, 1024)
        last = pre_buf[pl.ds(48, 16), low].astype(F32)[8:]
        last_high = pre_buf[pl.ds(48, 16), high].astype(F32)[8:]
        last = jnp.where(top, pltpu.roll(last, 4, 0), last_high)
        tail_out[part // 2, :, pl.ds((part % 2) * 1024, 1024)] = last
        first = []
        for buf in (pre_buf, act_buf):
            rows = buf[pl.ds(0, 16), low].astype(F32)[:8]
            rows_high = buf[pl.ds(0, 16), high].astype(F32)[:8]
            first.append(jnp.where(top, rows, pltpu.roll(rows_high, 4, 0)))
        head_out[:, low] = jnp.concatenate(first, axis=0).astype(BF16)
    params[me, pl.ds(0, TAPS), :] = taps_ref[...]
    params[me, pl.ds(TAPS, 1), :] = bias_ref[...]
    params[me, pl.ds(TAPS + 1, 3), :] = jnp.zeros((3, WIDTH), F32)

    pl.semaphore_wait(barrier, GROUP + 1)

    tail = remote(
        tail_out, tail_in, halo_send.at[0], halo_recv.at[0], (dp, group_peer(1))
    )
    head = remote(
        head_out, head_in, halo_send.at[1], halo_recv.at[1], (dp, group_peer(GROUP - 1))
    )
    tail.start()
    head.start()

    def share(step, _):
        remote(
            params.at[me], params.at[me], param_send, param_recv, (dp, group_peer(step))
        ).start()
        return 0

    lax.fori_loop(1, GROUP, share, 0)

    def weight_rows(q, half):
        return pl.ds(pl.multiple_of(q * CHUNK + half * (CHUNK // 2), CHUNK // 2), CHUNK // 2)

    def weight_copies(q):
        rows = weight_rows(q, core)
        return [
            remote(
                src.at[rows],
                right.at[rows, pl.ds(slot * WIDTH, WIDTH)],
                w_send.at[q, k],
                w_recv.at[q, k],
                outside,
            )
            for k, (src, slot) in enumerate(((upx_hbm, 1), (upz_hbm, 3)))
        ]

    def forward_copies(q):
        rows = weight_rows(q, core)
        return [
            remote(
                right.at[rows, pl.ds(slot * WIDTH, WIDTH)],
                right.at[rows, pl.ds(slot * WIDTH, WIDTH)],
                fwd_send.at[q, k],
                fwd_recv.at[q, k],
                sibling,
            )
            for k, slot in enumerate((1, 3))
        ]

    for q in range(CHUNKS):
        for copy in weight_copies(q):
            copy.start()

    def up_gradient(n, slot, turned, result):
        columns = pl.ds(pl.multiple_of(n * 512, 512), 512)
        rows = normed[:, :, :, columns].reshape(TOKENS, 512)
        product = jnp.dot(turned[...], rows, preferred_element_type=F32)
        stage[slot] = product.T
        local(stage.at[slot], result.at[columns], stage_sem.at[slot]).start()

    def stage_wait(slot):
        local(stage.at[slot], guz_hbm.at[pl.ds(0, 512)], stage_sem.at[slot]).wait()

    loads[2].wait()
    loads[3].wait()

    def turn_gate(b, _):
        near = left[b, :, pl.ds(2 * WIDTH, WIDTH)]
        pair = jnp.concatenate([near, gate_far[b]], axis=0).astype(F32)
        gate_t[:, pl.ds(pl.multiple_of(b * 128, 128), 128)] = pair.T.astype(BF16)
        return 0

    lax.fori_loop(0, 16, turn_gate, 0)

    tail.wait_recv()
    head.wait_recv()
    others = pl.ds(0, GROUP - 1)
    local(params.at[others], params.at[others], param_recv).wait()

    def convolve(i, _):
        g = (spot + i) % 16
        lower = g < 8
        for block in range(2):
            feature = 2 * g + (x + block) % 2
            for part in range(2):
                inner = pl.ds(part * 128, 128)
                lane = pl.multiple_of(feature * WIDTH + part * 128, 128)
                packed = pl.multiple_of((feature % 16) * WIDTH + part * 128, 128)
                lanes = pl.ds(lane, 128)
                weights = [params[feature, pl.ds(j, 1), inner] for j in range(TAPS)]
                bias = params[feature, pl.ds(TAPS, 1), inner]
                before = tail_in[
                    (feature % 16) // 8,
                    :,
                    pl.ds(pl.multiple_of((feature % 8) * WIDTH + part * 128, 128), 128),
                ]
                before = jnp.where(lower, pltpu.roll(before, 4, 0), before)
                before = jnp.where(me == 0, 0.0, before)
                after = head_in[:, pl.ds(packed, 128)].astype(F32)
                after_pre, after_act = after[:8], after[8:]
                after_pre = jnp.where(lower, after_pre, pltpu.roll(after_pre, 4, 0))
                after_act = jnp.where(lower, after_act, pltpu.roll(after_act, 4, 0))
                after_act = jnp.where(me == GROUP - 1, 0.0, after_act)
                window = jnp.concatenate(
                    [before, pre_buf[:, lanes].astype(F32), after_pre], axis=0
                )
                incoming = jnp.concatenate([act_buf[:, lanes].astype(F32), after_act], axis=0)
                shifted = [window[8:]] + [pltpu.roll(window, j, 0)[8:] for j in range(1, TAPS)]
                conv = bias + (
                    weights[0] * shifted[0]
                    + weights[1] * shifted[1]
                    + weights[2] * shifted[2]
                    + weights[3] * shifted[3]
                )
                sig = 1.0 / (1.0 + jnp.exp(-conv))
                cell = (incoming * sig * (1.0 + conv * (1.0 - sig))).astype(BF16).astype(F32)
                grad = weights[0] * cell[:ROWS]
                for j in range(1, TAPS):
                    grad += weights[j] * pltpu.roll(cell, 72 - j, 0)[:ROWS]
                gx_out[g, :, pl.ds(block * WIDTH + part * 128, 128)] = grad.astype(BF16)
                mine = cell[:ROWS]
                sums = [(shifted[j][:ROWS] * mine).sum(0, keepdims=True) for j in range(TAPS)]
                sums.append(mine.sum(0, keepdims=True))
                sums.append(jnp.zeros((3, 128), F32))
                sums_out[feature, :, inner] = jnp.concatenate(sums, axis=0)

        @pl.when(i < 16)
        def _():
            remote(
                gx_out.at[g],
                left.at[spot, :, pl.ds(0, 2 * WIDTH)],
                gx_send,
                gx_recv,
                (dp, 2 * g + x),
            ).start()

        return 0

    lax.fori_loop(1, 17, convolve, 0)
    own_gx = local(gx_out.at[spot], left.at[spot, :, pl.ds(0, 2 * WIDTH)], load_sem.at[0])
    own_gx.start()

    gate_pair = remote(
        gate_hbm.at[:, 1 - x],
        left.at[:, :, pl.ds(3 * WIDTH, WIDTH)],
        pair_send.at[0],
        pair_recv.at[0],
        partner,
    )
    gate_pair.start()

    loads[4].wait()
    loads[5].wait()

    def gate_step(n, _):
        for slot in range(2):

            @pl.when(n > 0)
            def _():
                stage_wait(slot)

            up_gradient(2 * n + slot, slot, gate_t, guz_hbm)
        return 0

    lax.fori_loop(0, 2, gate_step, 0)

    def forward(q):
        for copy in weight_copies(q):
            copy.wait_recv()
        for copy in forward_copies(q):
            copy.start()

    forward(0)

    def hand_sums(step, _):
        peer = group_peer(step)
        remote(
            sums_out.at[peer], sums_in.at[me], sums_send, sums_recv, (dp, peer)
        ).start()
        return 0

    def place(s, first):
        along_z = (1 - s) if first else s
        return along_z * z + (1 - along_z) * y

    def neighbour(s, first, step):
        along_z = (1 - s) if first else s
        far_z = (z + step * along_z) % 4
        far_y = (y + step * (1 - along_z)) % 4
        return (dp, (far_z * 4 + far_y) * 2 + x)

    def term(q, s, step, half):
        target = (place(s, True) + step) % 4
        base = target * (4 - 3 * s)
        stride = 1 + 3 * s
        rows = jnp.concatenate([left[base + stride * j] for j in range(4)], axis=0)
        columns = pl.ds(
            pl.multiple_of(q * CHUNK + s * (CHUNK // 2) + half * TILE, TILE), TILE
        )
        return lax.dot_general(
            rows, right[columns, :], (((1,), (1,)), ((), ())), preferred_element_type=F32
        )

    def hop1(q, s, k):
        step = 1 + 2 * (k % 2)
        return remote(
            send1.at[q, s, k],
            recv1.at[q, s, k],
            s1_send,
            s1_recv.at[q, s, k],
            neighbour(s, True, step),
        )

    def hop2(q, s, k):
        step = 1 + 2 * (k % 2)
        return remote(
            send2.at[q, s, k],
            recv2.at[q, s, k],
            s2_send,
            s2_recv.at[q, s, k],
            neighbour(s, False, step),
        )

    def first_terms(q):
        if q > 0:
            forward(q)
        for copy in forward_copies(q):
            copy.wait_recv()

        def body(i, _):
            k, s = i // 2, i % 2
            near = k // 2
            step = 2 - near + 2 * near * (k % 2)
            half = (k + near) % 2
            send1[q, s, k] = term(q, s, step, half).astype(BF16)
            hop1(q, s, k).start()
            return 0

        lax.fori_loop(0, 8, body, 0)

    def passed_terms(q):
        def body(i, _):
            half, s = i // 2, i % 2
            value = term(q, s, 1 + 2 * half, half)
            hop1(q, s, half).wait_recv()
            send1[q, s, 4 + half] = (value + recv1[q, s, half].astype(F32)).astype(BF16)
            hop1(q, s, 4 + half).start()
            return 0

        lax.fori_loop(0, 4, body, 0)

    def own_terms(q):
        def body(i, _):
            half, s = i // 2, i % 2
            value = term(q, s, 0, half)
            hop1(q, s, 4 - 2 * half).wait_recv()
            hop1(q, s, 3 + 2 * half).wait_recv()
            value += recv1[q, s, 4 - 2 * half].astype(F32)
            value += recv1[q, s, 3 + 2 * half].astype(F32)
            total[q, s, half] = value.reshape(4, ROWS, TILE)
            return 0

        lax.fori_loop(0, 4, body, 0)

        def spread(i, _):
            k, s = i // 2, i % 2
            near = k // 2
            step = 2 - near + 2 * near * (k % 2)
            half = (k + near) % 2
            send2[q, s, k] = total[q, s, half, (place(s, False) + step) % 4].astype(BF16)
            hop2(q, s, k).start()
            return 0

        lax.fori_loop(0, 8, spread, 0)

    def passed_rows(q):
        def body(i, _):
            half, s = i // 2, i % 2
            value = total[q, s, half, (place(s, False) + 1 + 2 * half) % 4]
            hop2(q, s, half).wait_recv()
            send2[q, s, 4 + half] = (value + recv2[q, s, half].astype(F32)).astype(BF16)
            hop2(q, s, 4 + half).start()
            return 0

        lax.fori_loop(0, 4, body, 0)

    def finish(q):
        for s in range(2):
            for half in range(2):
                value = total[q, s, half, place(s, False)]
                hop2(q, s, 4 - 2 * half).wait_recv()
                hop2(q, s, 3 + 2 * half).wait_recv()
                value += recv2[q, s, 4 - 2 * half].astype(F32)
                value += recv2[q, s, 3 + 2 * half].astype(F32)
                out_ref[:, pl.ds(q * CHUNK + s * (CHUNK // 2) + half * TILE, TILE)] = (
                    value.astype(BF16)
                )

    def turn_gx(b, _):
        pair = jnp.concatenate([left[b, :, pl.ds(0, WIDTH)], gx_far[b]], axis=0).astype(F32)
        gx_t[:, pl.ds(pl.multiple_of(b * 128, 128), 128)] = pair.T.astype(BF16)
        return 0

    def gx_step(n):
        for slot in range(2):
            stage_wait(slot)
            up_gradient(2 * n + slot, slot, gx_t, gux_hbm)

    loads[6].wait()
    loads[7].wait()
    own_gx.wait()
    far_spots = pl.ds(0, 15)
    local(gx_out.at[far_spots], gx_out.at[far_spots], gx_recv).wait()
    gx_pair = remote(
        left.at[:, :, pl.ds(WIDTH, WIDTH)], gx_far, pair_send.at[1], pair_recv.at[1], partner
    )
    gx_pair.start()
    gate_pair.wait_recv()

    first_terms(0)
    first_terms(1)
    lax.fori_loop(1, GROUP, hand_sums, 0)
    sums_in[me] = sums_out[me]
    passed_terms(0)
    first_terms(2)
    passed_terms(1)
    lax.fori_loop(2, 4, gate_step, 0)
    gx_pair.wait_recv()
    lax.fori_loop(0, 16, turn_gx, 0)
    gx_step(0)
    own_terms(0)
    first_terms(3)
    passed_terms(2)
    gx_step(1)
    own_terms(1)
    passed_rows(0)
    passed_terms(3)
    gx_step(2)
    own_terms(2)
    passed_rows(1)
    finish(0)
    gx_step(3)
    own_terms(3)
    passed_rows(2)
    finish(1)
    passed_rows(3)
    finish(2)
    finish(3)

    local(sums_in.at[others], sums_in.at[others], sums_recv).wait()
    small_ref[...] = sums_in[...].sum(0)

    tail.wait_send()
    head.wait_send()
    local(params.at[others], params.at[others], param_send).wait()
    local(sums_out.at[others], sums_out.at[others], sums_send).wait()
    local(gx_out.at[far_spots], gx_out.at[far_spots], gx_send).wait()
    gate_pair.wait_send()
    gx_pair.wait_send()
    for q in range(CHUNKS):
        for copy in weight_copies(q) + forward_copies(q):
            copy.wait_send()
    local(send1, send1, s1_send).wait()
    local(send2, send2, s2_send).wait()
    for slot in range(2):
        stage_wait(slot)


def per_device(grad_act, x_pre, grad_gate, normed_input, conv_weight, conv_bias, up_x, up_z):
    anywhere = pl.BlockSpec(memory_space=pl.ANY)
    vmem = pl.BlockSpec(memory_space=pltpu.VMEM)
    dma = pltpu.SemaphoreType.DMA
    out, gux, guz, small = pl.pallas_call(
        kernel,
        out_shape=(
            jax.ShapeDtypeStruct((ROWS, DIM), BF16),
            jax.ShapeDtypeStruct((DIM, WIDTH), F32),
            jax.ShapeDtypeStruct((DIM, WIDTH), F32),
            jax.ShapeDtypeStruct((8, WIDTH), F32),
        ),
        in_specs=[anywhere] * 4 + [vmem] * 2 + [anywhere] * 2,
        out_specs=(vmem, anywhere, anywhere, vmem),
        scratch_shapes=[
            pltpu.VMEM((ROWS, INNER), BF16),
            pltpu.VMEM((ROWS, INNER), BF16),
            pltpu.VMEM((2, 8, HALF // 2), F32),
            pltpu.VMEM((2, 8, HALF // 2), F32),
            pltpu.VMEM((16, HALF), BF16),
            pltpu.VMEM((16, HALF), BF16),
            pltpu.VMEM((GROUP, 8, WIDTH), F32),
            pltpu.VMEM((GROUP, 8, WIDTH), F32),
            pltpu.VMEM((GROUP, 8, WIDTH), F32),
            pltpu.VMEM((16, ROWS, WIDTH), BF16),
            pltpu.VMEM((WIDTH, TOKENS), BF16),
            pltpu.VMEM((16, ROWS, 2 * WIDTH), BF16),
            pltpu.VMEM((16, ROWS, WIDTH), BF16),
            pltpu.VMEM((WIDTH, TOKENS), BF16),
            pltpu.VMEM((16, ROWS, 4 * WIDTH), BF16),
            pltpu.VMEM((DIM, 4 * WIDTH), BF16),
            pltpu.VMEM((16, 2, ROWS, DIM), BF16),
            pltpu.VMEM((2, 512, WIDTH), F32),
            pltpu.VMEM((CHUNKS, 2, 6, 256, TILE), BF16),
            pltpu.VMEM((CHUNKS, 2, 6, 256, TILE), BF16),
            pltpu.VMEM((CHUNKS, 2, 6, ROWS, TILE), BF16),
            pltpu.VMEM((CHUNKS, 2, 6, ROWS, TILE), BF16),
            pltpu.VMEM((CHUNKS, 2, 2, 4, ROWS, TILE), F32),
            dma((8,)),
            dma,
            dma,
            dma((2,)),
            dma((2,)),
            dma,
            dma,
            dma,
            dma,
            dma((CHUNKS, 2)),
            dma((CHUNKS, 2)),
            dma((CHUNKS, 2)),
            dma((CHUNKS, 2)),
            dma((2,)),
            dma((2,)),
            dma((2,)),
            dma,
            dma((CHUNKS, 2, 6)),
            dma,
            dma((CHUNKS, 2, 6)),
        ],
        compiler_params=pltpu.CompilerParams(
            collective_id=0, has_side_effects=True, vmem_limit_bytes=62 * 1024 * 1024
        ),
        name="conv_up_backward",
    )(
        grad_act,
        x_pre,
        grad_gate.reshape(16, 2, ROWS, WIDTH),
        normed_input.reshape(16, 2, ROWS, DIM),
        conv_weight,
        conv_bias.reshape(1, WIDTH),
        up_x,
        up_z,
    )
    return out, gux, guz, small[:TAPS], small[TAPS]


def solution(mesh):
    placed = (
        P(("dp", "tensor"), None),
        P(("dp", "tensor"), None),
        P("dp", "tensor"),
        P("dp", None),
        P(None, "tensor"),
        P("tensor"),
        P(None, "tensor"),
        P(None, "tensor"),
    )
    return jax.shard_map(
        per_device,
        mesh=mesh,
        in_specs=placed,
        out_specs=(
            P(("dp", "tensor"), None),
            P("dp", "tensor"),
            P("dp", "tensor"),
            P("dp", "tensor"),
            P(("dp", "tensor")),
        ),
        check_vma=False,
    )
```

```python
import jax
import jax.numpy as jnp
from jax import lax
from jax.experimental import pallas as pl
from jax.experimental.pallas import tpu as pltpu
from jax.sharding import PartitionSpec as P

MESH = pl.DeviceIdType.MESH
F32 = jnp.float32
BF16 = jnp.bfloat16
TAPS = 4
GROUP = 32
ROWS = 64
WIDTH = 256
DIM = 4096
INNER = 8192
HALF = INNER // 2
TOKENS = GROUP * ROWS
CHUNKS = 4
CHUNK = DIM // CHUNKS
PIECES = 4
TILE = CHUNK // 4


def kernel(
    act_hbm,
    pre_hbm,
    gate_hbm,
    normed_hbm,
    taps_ref,
    bias_ref,
    upx_hbm,
    upz_hbm,
    out_ref,
    gux_hbm,
    guz_hbm,
    small_ref,
    act_buf,
    pre_buf,
    tail_out,
    tail_in,
    head_out,
    head_in,
    params,
    sums_out,
    sums_in,
    pair_out,
    pair_in,
    gate_far,
    gate_t,
    gx_out,
    gx_far,
    gx_t,
    left,
    right,
    normed,
    stage,
    send1,
    recv1,
    send2,
    recv2,
    total,
    load_sem,
    param_send,
    param_recv,
    halo_send,
    halo_recv,
    gx_send,
    gx_recv,
    sums_send,
    sums_recv,
    w_send,
    w_recv,
    fwd_send,
    fwd_recv,
    pair_send,
    pair_recv,
    stage_sem,
    s1_send,
    s1_recv,
    s2_send,
    s2_recv,
):
    dp = lax.axis_index("dp")
    me = lax.axis_index("tensor")
    z, y, x = me // 8, (me // 2) % 4, me % 2
    spot = me // 2
    core = dp % 2
    partner = (dp, me + 1 - 2 * x)
    outside = ((dp + 2) % 4, me + 1 - 2 * x)
    sibling = (dp + 1 - 2 * core, me)

    def same_x(step):
        return (dp, (spot + step) % 16 * 2 + x)

    def other_x(step):
        return (dp, (spot + step) % 16 * 2 + 1 - x)

    def local(src, dst, sem):
        return pltpu.make_async_copy(src, dst, sem)

    def remote(src, dst, send, recv, device):
        return pltpu.make_async_remote_copy(
            src_ref=src,
            dst_ref=dst,
            send_sem=send,
            recv_sem=recv,
            device_id=device,
            device_id_type=MESH,
        )

    loads = [
        local(pre_hbm, pre_buf, load_sem.at[0]),
        local(act_hbm, act_buf, load_sem.at[1]),
        local(gate_hbm.at[:, x], left.at[:, :, pl.ds(2 * WIDTH, WIDTH)], load_sem.at[2]),
        local(gate_hbm.at[:, 1 - x], gate_far, load_sem.at[3]),
        local(normed_hbm.at[:, x], normed.at[:, 0], load_sem.at[4]),
        local(normed_hbm.at[:, 1 - x], normed.at[:, 1], load_sem.at[5]),
        local(upx_hbm, right.at[:, pl.ds(0, WIDTH)], load_sem.at[6]),
        local(upz_hbm, right.at[:, pl.ds(2 * WIDTH, WIDTH)], load_sem.at[7]),
    ]
    for copy in loads:
        copy.start()

    barrier = pltpu.get_barrier_semaphore()

    def greet(device):
        pl.semaphore_signal(barrier, inc=1, device_id=device, device_id_type=MESH)

    def greet_step(step, _):
        greet(same_x(step))
        greet(other_x(step))
        return 0

    greet(partner)
    greet(sibling)
    greet(outside)
    lax.fori_loop(1, 16, greet_step, 0)

    loads[0].wait()
    loads[1].wait()
    top = lax.broadcasted_iota(jnp.int32, (8, 1024), 0) < 4
    for part in range(2):
        last = []
        for k in (part, part + 2):
            low = pre_buf[pl.ds(48, 16), pl.ds(k * 1024, 1024)].astype(F32)[8:]
            high = pre_buf[pl.ds(48, 16), pl.ds(HALF + k * 1024, 1024)].astype(F32)[8:]
            last.append(jnp.where(top, pltpu.roll(low, 4, 0), high))
        tail_out[:, pl.ds(part * 1024, 1024)] = jnp.concatenate(last, axis=0).astype(BF16)
    for part in range(4):
        first = []
        for buf in (pre_buf, act_buf):
            low = buf[pl.ds(0, 16), pl.ds(part * 1024, 1024)].astype(F32)[:8]
            high = buf[pl.ds(0, 16), pl.ds(HALF + part * 1024, 1024)].astype(F32)[:8]
            first.append(jnp.where(top, low, pltpu.roll(high, 4, 0)))
        head_out[:, pl.ds(part * 1024, 1024)] = jnp.concatenate(first, axis=0).astype(BF16)
    params[me, pl.ds(0, TAPS), :] = taps_ref[...]
    params[me, pl.ds(TAPS, 1), :] = bias_ref[...]
    params[me, pl.ds(TAPS + 1, 3), :] = jnp.zeros((3, WIDTH), F32)

    pl.semaphore_wait(barrier, GROUP + 1)

    after_me = (dp, (me + 1) % GROUP)
    before_me = (dp, (me + GROUP - 1) % GROUP)
    tail = remote(tail_out, tail_in, halo_send.at[0], halo_recv.at[0], after_me)
    head = remote(head_out, head_in, halo_send.at[1], halo_recv.at[1], before_me)
    tail.start()
    head.start()

    def share_with(device):
        remote(params.at[me], params.at[me], param_send, param_recv, device).start()

    def share(step, _):
        share_with(same_x(step))
        share_with(other_x(step))
        return 0

    lax.fori_loop(1, 16, share, 0)
    share_with(partner)

    gate_pair = remote(
        gate_hbm.at[:, 1 - x],
        left.at[:, :, pl.ds(3 * WIDTH, WIDTH)],
        pair_send.at[0],
        pair_recv.at[0],
        partner,
    )
    gate_pair.start()

    def weight_rows(q, half):
        return pl.ds(pl.multiple_of(q * CHUNK + half * (CHUNK // 2), CHUNK // 2), CHUNK // 2)

    def weight_copies(q):
        rows = weight_rows(q, core)
        return [
            remote(
                src.at[rows],
                right.at[rows, pl.ds(slot * WIDTH, WIDTH)],
                w_send.at[q, k],
                w_recv.at[q, k],
                outside if q < CHUNKS - 1 else partner,
            )
            for k, (src, slot) in enumerate(((upx_hbm, 1), (upz_hbm, 3)))
        ]

    def forward_copies(q):
        rows = weight_rows(q, core)
        return [
            remote(
                right.at[rows, pl.ds(slot * WIDTH, WIDTH)],
                right.at[rows, pl.ds(slot * WIDTH, WIDTH)],
                fwd_send.at[q, k],
                fwd_recv.at[q, k],
                sibling,
            )
            for k, slot in enumerate((1, 3))
        ]

    for q in range(CHUNKS):
        for copy in weight_copies(q):
            copy.start()

    def up_gradient(n, slot, turned, result):
        columns = pl.ds(pl.multiple_of(n * 512, 512), 512)
        rows = normed[:, :, :, columns].reshape(TOKENS, 512)
        product = jnp.dot(turned[...], rows, preferred_element_type=F32)
        stage[slot] = product.T
        local(stage.at[slot], result.at[columns], stage_sem.at[slot]).start()

    def stage_wait(slot):
        local(stage.at[slot], guz_hbm.at[pl.ds(0, 512)], stage_sem.at[slot]).wait()

    loads[2].wait()
    loads[3].wait()

    def turn_gate(b, _):
        near = left[b, :, pl.ds(2 * WIDTH, WIDTH)]
        pair = jnp.concatenate([near, gate_far[b]], axis=0).astype(F32)
        gate_t[:, pl.ds(pl.multiple_of(b * 128, 128), 128)] = pair.T.astype(BF16)
        return 0

    lax.fori_loop(0, 16, turn_gate, 0)

    tail.wait_recv()
    head.wait_recv()
    others = pl.ds(0, GROUP - 1)
    local(params.at[others], params.at[others], param_recv).wait()

    def skip_two(v):
        return v + v // 2

    def convolve(n, _):
        rest = 15 - n
        dz = jnp.where(n < 4, 2, jnp.where(n < 7, skip_two(n - 4), skip_two(rest // 3)))
        dy = jnp.where(n < 4, n, jnp.where(n < 7, 2, skip_two(rest % 3)))
        g = (z + dz) % 4 * 4 + (y + dy) % 4
        lower = g < 8
        for block in range(2):
            feature = 2 * g + (x + block) % 2
            for part in range(2):
                inner = pl.ds(part * 128, 128)
                lane = pl.multiple_of(feature * WIDTH + part * 128, 128)
                packed = pl.multiple_of((feature % 16) * WIDTH + part * 128, 128)
                lanes = pl.ds(lane, 128)
                weights = [params[feature, pl.ds(j, 1), inner] for j in range(TAPS)]
                bias = params[feature, pl.ds(TAPS, 1), inner]
                before = tail_in[
                    :, pl.ds(pl.multiple_of((feature % 8) * WIDTH + part * 128, 128), 128)
                ].astype(F32)
                before = jnp.where((feature % 16) < 8, before[:8], before[8:])
                before = jnp.where(lower, pltpu.roll(before, 4, 0), before)
                before = jnp.where(me == 0, 0.0, before)
                after = head_in[:, pl.ds(packed, 128)].astype(F32)
                after_pre, after_act = after[:8], after[8:]
                after_pre = jnp.where(lower, after_pre, pltpu.roll(after_pre, 4, 0))
                after_act = jnp.where(lower, after_act, pltpu.roll(after_act, 4, 0))
                after_act = jnp.where(me == GROUP - 1, 0.0, after_act)
                window = jnp.concatenate(
                    [before, pre_buf[:, lanes].astype(F32), after_pre], axis=0
                )
                incoming = jnp.concatenate([act_buf[:, lanes].astype(F32), after_act], axis=0)
                shifted = [window[8:]] + [pltpu.roll(window, j, 0)[8:] for j in range(1, TAPS)]
                conv = bias + (
                    weights[0] * shifted[0]
                    + weights[1] * shifted[1]
                    + weights[2] * shifted[2]
                    + weights[3] * shifted[3]
                )
                sig = 1.0 / (1.0 + jnp.exp(-conv))
                cell = (incoming * sig * (1.0 + conv * (1.0 - sig))).astype(BF16).astype(F32)
                grad = weights[0] * cell[:ROWS]
                for j in range(1, TAPS):
                    grad += weights[j] * pltpu.roll(cell, 72 - j, 0)[:ROWS]
                gx_out[g, :, pl.ds(block * WIDTH + part * 128, 128)] = grad.astype(BF16)
                mine = cell[:ROWS]
                sums = [(shifted[j][:ROWS] * mine).sum(0, keepdims=True) for j in range(TAPS)]
                sums.append(mine.sum(0, keepdims=True))
                sums.append(jnp.zeros((3, 128), F32))
                sums_out[g, block, :, inner] = jnp.concatenate(sums, axis=0)

        @pl.when(n < 15)
        def _():
            remote(
                gx_out.at[g],
                left.at[spot, :, pl.ds(0, 2 * WIDTH)],
                gx_send,
                gx_recv.at[spot],
                (dp, 2 * g + x),
            ).start()

        return 0

    lax.fori_loop(0, 16, convolve, 0)
    own_gx = local(gx_out.at[spot], left.at[spot, :, pl.ds(0, 2 * WIDTH)], load_sem.at[0])
    own_gx.start()

    loads[4].wait()
    loads[5].wait()

    def gate_step(n, _):
        for slot in range(2):

            @pl.when(n > 0)
            def _():
                stage_wait(slot)

            up_gradient(2 * n + slot, slot, gate_t, guz_hbm)
        return 0

    lax.fori_loop(0, 2, gate_step, 0)

    def forward(q):
        for copy in weight_copies(q):
            copy.wait_recv()
        for copy in forward_copies(q):
            copy.start()

    forward(0)

    def hand_sums(step, _):
        device = same_x(step)
        remote(
            sums_out.at[(spot + step) % 16], sums_in.at[spot], sums_send, sums_recv, device
        ).start()
        return 0

    sums_pair = remote(pair_out, pair_in, pair_send.at[2], pair_recv.at[2], partner)

    def place(s, first):
        along_z = (1 - s) if first else s
        return along_z * z + (1 - along_z) * y

    def neighbour(s, first, step):
        along_z = (1 - s) if first else s
        far_z = (z + step * along_z) % 4
        far_y = (y + step * (1 - along_z)) % 4
        return (dp, (far_z * 4 + far_y) * 2 + x)

    def term(q, s, step, half):
        target = (place(s, True) + step) % 4
        base = target * (4 - 3 * s)
        stride = 1 + 3 * s
        rows = jnp.concatenate([left[base + stride * j] for j in range(4)], axis=0)
        columns = pl.ds(
            pl.multiple_of(q * CHUNK + s * (CHUNK // 2) + half * TILE, TILE), TILE
        )
        return lax.dot_general(
            rows, right[columns, :], (((1,), (1,)), ((), ())), preferred_element_type=F32
        )

    def hop1(q, s, k):
        step = 1 + 2 * (k % 2)
        return remote(
            send1.at[q, s, k],
            recv1.at[q, s, k],
            s1_send,
            s1_recv.at[q, s, k],
            neighbour(s, True, step),
        )

    def hop2(q, s, k):
        step = 1 + 2 * (k % 2)
        return remote(
            send2.at[q, s, k],
            recv2.at[q, s, k],
            s2_send,
            s2_recv.at[q, s, k],
            neighbour(s, False, step),
        )

    def gx_arrived(dz, dy):
        source = (z + dz) % 4 * 4 + (y + dy) % 4
        block = left.at[source, :, pl.ds(0, 2 * WIDTH)]
        local(block, block, gx_recv.at[source]).wait()

    def first_terms(q):
        for copy in forward_copies(q):
            copy.wait_recv()

        def body(i, _):
            k, s = i // 2, i % 2
            near = k // 2
            step = 2 - near + 2 * near * (k % 2)
            half = (k + near) % 2
            send1[q, s, k] = term(q, s, step, half).astype(BF16)
            hop1(q, s, k).start()
            return 0

        if q > 0:
            lax.fori_loop(0, 8, body, 0)
            return
        for dy in range(4):
            gx_arrived(2, dy)
        lax.fori_loop(0, 2, lambda i, _: body(2 * i, _), 0)
        for dz in (0, 1, 3):
            gx_arrived(dz, 2)
        lax.fori_loop(0, 2, lambda i, _: body(2 * i + 1, _), 0)
        own_gx.wait()
        for dz in (0, 1, 3):
            for dy in (0, 1, 3):
                if dz or dy:
                    gx_arrived(dz, dy)
        gx_pair.start()
        lax.fori_loop(4, 8, body, 0)

    def passed_terms(q):
        def body(i, _):
            half, s = i // 2, i % 2
            value = term(q, s, 1 + 2 * half, half)
            hop1(q, s, half).wait_recv()
            send1[q, s, 4 + half] = (value + recv1[q, s, half].astype(F32)).astype(BF16)
            hop1(q, s, 4 + half).start()
            return 0

        lax.fori_loop(0, 4, body, 0)

    def own_terms(q):
        def body(i, _):
            half, s = i // 2, i % 2
            value = term(q, s, 0, half)
            hop1(q, s, 4 - 2 * half).wait_recv()
            hop1(q, s, 3 + 2 * half).wait_recv()
            value += recv1[q, s, 4 - 2 * half].astype(F32)
            value += recv1[q, s, 3 + 2 * half].astype(F32)
            total[q, s, half] = value.reshape(4, ROWS, TILE)
            return 0

        lax.fori_loop(0, 4, body, 0)

        def spread(i, _):
            k, s = i // 2, i % 2
            near = k // 2
            step = 2 - near + 2 * near * (k % 2)
            half = (k + near) % 2
            send2[q, s, k] = total[q, s, half, (place(s, False) + step) % 4].astype(BF16)
            hop2(q, s, k).start()
            return 0

        lax.fori_loop(0, 8, spread, 0)

    def passed_rows(q):
        def body(i, _):
            half, s = i // 2, i % 2
            value = total[q, s, half, (place(s, False) + 1 + 2 * half) % 4]
            hop2(q, s, half).wait_recv()
            send2[q, s, 4 + half] = (value + recv2[q, s, half].astype(F32)).astype(BF16)
            hop2(q, s, 4 + half).start()
            return 0

        lax.fori_loop(0, 4, body, 0)

    def finish(q):
        for s in range(2):
            for half in range(2):
                value = total[q, s, half, place(s, False)]
                hop2(q, s, 4 - 2 * half).wait_recv()
                hop2(q, s, 3 + 2 * half).wait_recv()
                value += recv2[q, s, 4 - 2 * half].astype(F32)
                value += recv2[q, s, 3 + 2 * half].astype(F32)
                out_ref[:, pl.ds(q * CHUNK + s * (CHUNK // 2) + half * TILE, TILE)] = (
                    value.astype(BF16)
                )

    def turn_gx(b, _):
        pair = jnp.concatenate([left[b, :, pl.ds(0, WIDTH)], gx_far[b]], axis=0).astype(F32)
        gx_t[:, pl.ds(pl.multiple_of(b * 128, 128), 128)] = pair.T.astype(BF16)
        return 0

    def gx_step(n):
        for slot in range(2):
            stage_wait(slot)
            up_gradient(2 * n + slot, slot, gx_t, gux_hbm)

    loads[6].wait()
    loads[7].wait()
    far_spots = pl.ds(0, 15)
    gx_pair = remote(
        left.at[:, :, pl.ds(WIDTH, WIDTH)], gx_far, pair_send.at[1], pair_recv.at[1], partner
    )
    gate_pair.wait_recv()

    first_terms(0)
    forward(1)
    first_terms(1)
    lax.fori_loop(1, 16, hand_sums, 0)
    sums_in[spot] = sums_out[spot]
    passed_terms(0)
    forward(2)
    forward(3)
    lax.fori_loop(2, 4, gate_step, 0)
    first_terms(2)
    passed_terms(1)
    gx_pair.wait_recv()
    lax.fori_loop(0, 16, turn_gx, 0)
    gx_step(0)
    own_terms(0)
    first_terms(3)
    passed_terms(2)
    gx_step(1)
    own_terms(1)
    passed_rows(0)
    passed_terms(3)
    gx_step(2)
    local(sums_in.at[far_spots], sums_in.at[far_spots], sums_recv).wait()
    small_ref[...] = sums_in[:, 0].sum(0)
    pair_out[...] = sums_in[:, 1].sum(0)
    sums_pair.start()
    own_terms(2)
    passed_rows(1)
    finish(0)
    gx_step(3)
    own_terms(3)
    passed_rows(2)
    finish(1)
    passed_rows(3)
    finish(2)
    finish(3)

    sums_pair.wait_recv()
    small_ref[...] = small_ref[...] + pair_in[...]

    tail.wait_send()
    head.wait_send()
    local(params.at[others], params.at[others], param_send).wait()
    local(sums_out.at[far_spots], sums_out.at[far_spots], sums_send).wait()
    sums_pair.wait_send()
    local(gx_out.at[far_spots], gx_out.at[far_spots], gx_send).wait()
    gate_pair.wait_send()
    gx_pair.wait_send()
    for q in range(CHUNKS):
        for copy in weight_copies(q) + forward_copies(q):
            copy.wait_send()
    local(send1, send1, s1_send).wait()
    local(send2, send2, s2_send).wait()
    for slot in range(2):
        stage_wait(slot)


def deliver(
    rows_ref, gux_ref, guz_ref, small_ref, rows_out, gux_out, guz_out, taps_out, bias_out, hold, sem
):
    pieces = PIECES
    depth = DIM // pieces
    pairs = []
    for k in range(pieces):
        part = pl.ds(k * depth, depth)
        pairs.append((gux_ref.at[part], hold.at[0, part], gux_out.at[part]))
        pairs.append((guz_ref.at[part], hold.at[1, part], guz_out.at[part]))
    reads = [
        pltpu.make_async_copy(src, mid, sem.at[0, k]) for k, (src, mid, _) in enumerate(pairs)
    ]
    writes = [
        pltpu.make_async_copy(mid, dst, sem.at[1, k]) for k, (_, mid, dst) in enumerate(pairs)
    ]
    for copy in reads:
        copy.start()
    small = [
        pltpu.make_async_copy(src, dst, sem.at[k, 2 * pieces])
        for k, (src, dst) in enumerate(
            (
                (rows_ref, rows_out),
                (small_ref.at[pl.ds(0, TAPS)], taps_out),
                (small_ref.at[pl.ds(TAPS, 1)], bias_out),
            )
        )
    ]
    for copy in small:
        copy.start()
    for read, write in zip(reads, writes):
        read.wait()
        write.start()
    for copy in writes + small:
        copy.wait()


def per_device(grad_act, x_pre, grad_gate, normed_input, conv_weight, conv_bias, up_x, up_z):
    anywhere = pl.BlockSpec(memory_space=pl.ANY)
    vmem = pl.BlockSpec(memory_space=pltpu.VMEM)
    dma = pltpu.SemaphoreType.DMA
    out, gux, guz, small = pl.pallas_call(
        kernel,
        out_shape=(
            jax.ShapeDtypeStruct((ROWS, DIM), BF16),
            jax.ShapeDtypeStruct((DIM, WIDTH), F32),
            jax.ShapeDtypeStruct((DIM, WIDTH), F32),
            jax.ShapeDtypeStruct((8, WIDTH), F32),
        ),
        in_specs=[anywhere] * 4 + [vmem] * 2 + [anywhere] * 2,
        out_specs=(vmem, anywhere, anywhere, vmem),
        scratch_shapes=[
            pltpu.VMEM((ROWS, INNER), BF16),
            pltpu.VMEM((ROWS, INNER), BF16),
            pltpu.VMEM((16, HALF // 2), BF16),
            pltpu.VMEM((16, HALF // 2), BF16),
            pltpu.VMEM((16, HALF), BF16),
            pltpu.VMEM((16, HALF), BF16),
            pltpu.VMEM((GROUP, 8, WIDTH), F32),
            pltpu.VMEM((16, 2, 8, WIDTH), F32),
            pltpu.VMEM((16, 2, 8, WIDTH), F32),
            pltpu.VMEM((8, WIDTH), F32),
            pltpu.VMEM((8, WIDTH), F32),
            pltpu.VMEM((16, ROWS, WIDTH), BF16),
            pltpu.VMEM((WIDTH, TOKENS), BF16),
            pltpu.VMEM((16, ROWS, 2 * WIDTH), BF16),
            pltpu.VMEM((16, ROWS, WIDTH), BF16),
            pltpu.VMEM((WIDTH, TOKENS), BF16),
            pltpu.VMEM((16, ROWS, 4 * WIDTH), BF16),
            pltpu.VMEM((DIM, 4 * WIDTH), BF16),
            pltpu.VMEM((16, 2, ROWS, DIM), BF16),
            pltpu.VMEM((2, 512, WIDTH), F32),
            pltpu.VMEM((CHUNKS, 2, 6, 256, TILE), BF16),
            pltpu.VMEM((CHUNKS, 2, 6, 256, TILE), BF16),
            pltpu.VMEM((CHUNKS, 2, 6, ROWS, TILE), BF16),
            pltpu.VMEM((CHUNKS, 2, 6, ROWS, TILE), BF16),
            pltpu.VMEM((CHUNKS, 2, 2, 4, ROWS, TILE), F32),
            dma((8,)),
            dma,
            dma,
            dma((2,)),
            dma((2,)),
            dma,
            dma((16,)),
            dma,
            dma,
            dma((CHUNKS, 2)),
            dma((CHUNKS, 2)),
            dma((CHUNKS, 2)),
            dma((CHUNKS, 2)),
            dma((3,)),
            dma((3,)),
            dma((2,)),
            dma,
            dma((CHUNKS, 2, 6)),
            dma,
            dma((CHUNKS, 2, 6)),
        ],
        compiler_params=pltpu.CompilerParams(
            collective_id=0, has_side_effects=True, vmem_limit_bytes=62 * 1024 * 1024
        ),
        name="conv_up_backward",
    )(
        grad_act,
        x_pre,
        grad_gate.reshape(16, 2, ROWS, WIDTH),
        normed_input.reshape(16, 2, ROWS, DIM),
        conv_weight,
        conv_bias.reshape(1, WIDTH),
        up_x,
        up_z,
    )
    out, gux, guz, taps, bias = pl.pallas_call(
        deliver,
        out_shape=(
            jax.ShapeDtypeStruct((ROWS, DIM), BF16),
            jax.ShapeDtypeStruct((DIM, WIDTH), F32),
            jax.ShapeDtypeStruct((DIM, WIDTH), F32),
            jax.ShapeDtypeStruct((TAPS, WIDTH), F32),
            jax.ShapeDtypeStruct((1, WIDTH), F32),
        ),
        in_specs=[vmem, anywhere, anywhere, vmem],
        out_specs=(anywhere,) * 5,
        scratch_shapes=[pltpu.VMEM((2, DIM, WIDTH), F32), dma((3, 2 * PIECES + 1))],
        compiler_params=pltpu.CompilerParams(vmem_limit_bytes=62 * 1024 * 1024),
        name="deliver",
    )(out, gux, guz, small)
    return out, gux, guz, taps, bias.reshape(WIDTH)


def solution(mesh):
    placed = (
        P(("dp", "tensor"), None),
        P(("dp", "tensor"), None),
        P("dp", "tensor"),
        P("dp", None),
        P(None, "tensor"),
        P("tensor"),
        P(None, "tensor"),
        P(None, "tensor"),
    )
    return jax.shard_map(
        per_device,
        mesh=mesh,
        in_specs=placed,
        out_specs=(
            P(("dp", "tensor"), None),
            P("dp", "tensor"),
            P("dp", "tensor"),
            P("dp", "tensor"),
            P(("dp", "tensor")),
        ),
        check_vma=False,
    )
```

```python
import jax
import jax.numpy as jnp
from jax import lax
from jax.experimental import pallas as pl
from jax.experimental.pallas import tpu as pltpu
from jax.sharding import PartitionSpec as P

MESH = pl.DeviceIdType.MESH
F32 = jnp.float32
BF16 = jnp.bfloat16
TAPS = 4
GROUP = 32
ROWS = 64
WIDTH = 256
DIM = 4096
INNER = 8192
HALF = INNER // 2
TOKENS = GROUP * ROWS
CHUNKS = 4
CHUNK = DIM // CHUNKS
PIECES = 4
TILE = CHUNK // 4


def kernel(
    act_hbm,
    pre_hbm,
    gate_hbm,
    normed_hbm,
    taps_hbm,
    bias_hbm,
    upx_hbm,
    upz_hbm,
    out_hbm,
    gux_hbm,
    guz_hbm,
    small_ref,
    taps_buf,
    bias_buf,
    out_buf,
    act_buf,
    pre_buf,
    tail_out,
    tail_in,
    head_out,
    head_in,
    params,
    sums_out,
    sums_in,
    pair_out,
    pair_in,
    gate_far,
    gate_t,
    gx_out,
    gx_far,
    gx_t,
    left,
    right,
    normed,
    stage,
    send1,
    recv1,
    send2,
    recv2,
    total,
    load_sem,
    out_sem,
    param_send,
    param_recv,
    halo_send,
    halo_recv,
    gx_send,
    gx_recv,
    sums_send,
    sums_recv,
    w_send,
    w_recv,
    fwd_send,
    fwd_recv,
    pair_send,
    pair_recv,
    stage_sem,
    s1_send,
    s1_recv,
    s2_send,
    s2_recv,
):
    dp = lax.axis_index("dp")
    me = lax.axis_index("tensor")
    z, y, x = me // 8, (me // 2) % 4, me % 2
    spot = me // 2
    core = dp % 2
    partner = (dp, me + 1 - 2 * x)
    outside = ((dp + 2) % 4, me + 1 - 2 * x)
    sibling = (dp + 1 - 2 * core, me)

    def same_x(step):
        return (dp, (spot + step) % 16 * 2 + x)

    def other_x(step):
        return (dp, (spot + step) % 16 * 2 + 1 - x)

    def local(src, dst, sem):
        return pltpu.make_async_copy(src, dst, sem)

    def remote(src, dst, send, recv, device):
        return pltpu.make_async_remote_copy(
            src_ref=src,
            dst_ref=dst,
            send_sem=send,
            recv_sem=recv,
            device_id=device,
            device_id_type=MESH,
        )

    loads = [
        local(pre_hbm, pre_buf, load_sem.at[0]),
        local(act_hbm, act_buf, load_sem.at[1]),
        local(gate_hbm.at[:, x], left.at[:, :, pl.ds(2 * WIDTH, WIDTH)], load_sem.at[2]),
        local(gate_hbm.at[:, 1 - x], gate_far, load_sem.at[3]),
        local(normed_hbm.at[:, x], normed.at[:, 0], load_sem.at[4]),
        local(normed_hbm.at[:, 1 - x], normed.at[:, 1], load_sem.at[5]),
        local(upx_hbm, right.at[:, pl.ds(0, WIDTH)], load_sem.at[6]),
        local(upz_hbm, right.at[:, pl.ds(2 * WIDTH, WIDTH)], load_sem.at[7]),
        local(taps_hbm, taps_buf, load_sem.at[8]),
        local(bias_hbm, bias_buf, load_sem.at[9]),
    ]
    for copy in loads[8:] + loads[:8]:
        copy.start()

    barrier = pltpu.get_barrier_semaphore()

    def greet(device):
        pl.semaphore_signal(barrier, inc=1, device_id=device, device_id_type=MESH)

    def greet_step(step, _):
        greet(same_x(step))
        greet(other_x(step))
        return 0

    greet(partner)
    greet(sibling)
    greet(outside)
    lax.fori_loop(1, 16, greet_step, 0)

    loads[0].wait()
    loads[1].wait()
    top = lax.broadcasted_iota(jnp.int32, (8, 1024), 0) < 4
    for part in range(2):
        last = []
        for k in (part, part + 2):
            low = pre_buf[pl.ds(48, 16), pl.ds(k * 1024, 1024)].astype(F32)[8:]
            high = pre_buf[pl.ds(48, 16), pl.ds(HALF + k * 1024, 1024)].astype(F32)[8:]
            last.append(jnp.where(top, pltpu.roll(low, 4, 0), high))
        tail_out[:, pl.ds(part * 1024, 1024)] = jnp.concatenate(last, axis=0).astype(BF16)
    for part in range(4):
        first = []
        for buf in (pre_buf, act_buf):
            low = buf[pl.ds(0, 16), pl.ds(part * 1024, 1024)].astype(F32)[:8]
            high = buf[pl.ds(0, 16), pl.ds(HALF + part * 1024, 1024)].astype(F32)[:8]
            first.append(jnp.where(top, low, pltpu.roll(high, 4, 0)))
        head_out[:, pl.ds(part * 1024, 1024)] = jnp.concatenate(first, axis=0).astype(BF16)
    loads[8].wait()
    loads[9].wait()
    params[me, pl.ds(0, TAPS), :] = taps_buf[...]
    params[me, pl.ds(TAPS, 1), :] = bias_buf[...]
    params[me, pl.ds(TAPS + 1, 3), :] = jnp.zeros((3, WIDTH), F32)

    pl.semaphore_wait(barrier, GROUP + 1)

    after_me = (dp, (me + 1) % GROUP)
    before_me = (dp, (me + GROUP - 1) % GROUP)
    tail = remote(tail_out, tail_in, halo_send.at[0], halo_recv.at[0], after_me)
    head = remote(head_out, head_in, halo_send.at[1], halo_recv.at[1], before_me)
    tail.start()
    head.start()

    def share_with(device):
        remote(params.at[me], params.at[me], param_send, param_recv, device).start()

    def share(step, _):
        share_with(same_x(step))
        share_with(other_x(step))
        return 0

    lax.fori_loop(1, 16, share, 0)
    share_with(partner)

    gate_pair = remote(
        gate_hbm.at[:, 1 - x],
        left.at[:, :, pl.ds(3 * WIDTH, WIDTH)],
        pair_send.at[0],
        pair_recv.at[0],
        partner,
    )
    gate_pair.start()

    def weight_rows(q, half):
        return pl.ds(pl.multiple_of(q * CHUNK + half * (CHUNK // 2), CHUNK // 2), CHUNK // 2)

    def weight_copies(q):
        rows = weight_rows(q, core)
        return [
            remote(
                src.at[rows],
                right.at[rows, pl.ds(slot * WIDTH, WIDTH)],
                w_send.at[q, k],
                w_recv.at[q, k],
                outside if q < CHUNKS - 1 else partner,
            )
            for k, (src, slot) in enumerate(((upx_hbm, 1), (upz_hbm, 3)))
        ]

    def forward_copies(q):
        rows = weight_rows(q, core)
        return [
            remote(
                right.at[rows, pl.ds(slot * WIDTH, WIDTH)],
                right.at[rows, pl.ds(slot * WIDTH, WIDTH)],
                fwd_send.at[q, k],
                fwd_recv.at[q, k],
                sibling,
            )
            for k, slot in enumerate((1, 3))
        ]

    for q in range(CHUNKS):
        for copy in weight_copies(q):
            copy.start()

    def up_gradient(n, slot, turned, result):
        columns = pl.ds(pl.multiple_of(n * 512, 512), 512)
        rows = normed[:, :, :, columns].reshape(TOKENS, 512)
        product = jnp.dot(turned[...], rows, preferred_element_type=F32)
        stage[slot] = product.T
        local(stage.at[slot], result.at[columns], stage_sem.at[slot]).start()

    def stage_wait(slot):
        local(stage.at[slot], guz_hbm.at[pl.ds(0, 512)], stage_sem.at[slot]).wait()

    loads[2].wait()
    loads[3].wait()

    def turn_gate(b, _):
        near = left[b, :, pl.ds(2 * WIDTH, WIDTH)]
        pair = jnp.concatenate([near, gate_far[b]], axis=0).astype(F32)
        gate_t[:, pl.ds(pl.multiple_of(b * 128, 128), 128)] = pair.T.astype(BF16)
        return 0

    lax.fori_loop(0, 16, turn_gate, 0)

    tail.wait_recv()
    head.wait_recv()
    others = pl.ds(0, GROUP - 1)
    local(params.at[others], params.at[others], param_recv).wait()

    def skip_two(v):
        return v + v // 2

    def convolve(n, _):
        rest = 15 - n
        dz = jnp.where(n < 4, 2, jnp.where(n < 7, skip_two(n - 4), skip_two(rest // 3)))
        dy = jnp.where(n < 4, n, jnp.where(n < 7, 2, skip_two(rest % 3)))
        g = (z + dz) % 4 * 4 + (y + dy) % 4
        lower = g < 8
        for block in range(2):
            feature = 2 * g + (x + block) % 2
            for part in range(2):
                inner = pl.ds(part * 128, 128)
                lane = pl.multiple_of(feature * WIDTH + part * 128, 128)
                packed = pl.multiple_of((feature % 16) * WIDTH + part * 128, 128)
                lanes = pl.ds(lane, 128)
                weights = [params[feature, pl.ds(j, 1), inner] for j in range(TAPS)]
                bias = params[feature, pl.ds(TAPS, 1), inner]
                before = tail_in[
                    :, pl.ds(pl.multiple_of((feature % 8) * WIDTH + part * 128, 128), 128)
                ].astype(F32)
                before = jnp.where((feature % 16) < 8, before[:8], before[8:])
                before = jnp.where(lower, pltpu.roll(before, 4, 0), before)
                before = jnp.where(me == 0, 0.0, before)
                after = head_in[:, pl.ds(packed, 128)].astype(F32)
                after_pre, after_act = after[:8], after[8:]
                after_pre = jnp.where(lower, after_pre, pltpu.roll(after_pre, 4, 0))
                after_act = jnp.where(lower, after_act, pltpu.roll(after_act, 4, 0))
                after_act = jnp.where(me == GROUP - 1, 0.0, after_act)
                window = jnp.concatenate(
                    [before, pre_buf[:, lanes].astype(F32), after_pre], axis=0
                )
                incoming = jnp.concatenate([act_buf[:, lanes].astype(F32), after_act], axis=0)
                shifted = [window[8:]] + [pltpu.roll(window, j, 0)[8:] for j in range(1, TAPS)]
                conv = bias + (
                    weights[0] * shifted[0]
                    + weights[1] * shifted[1]
                    + weights[2] * shifted[2]
                    + weights[3] * shifted[3]
                )
                sig = 1.0 / (1.0 + jnp.exp(-conv))
                cell = (incoming * sig * (1.0 + conv * (1.0 - sig))).astype(BF16).astype(F32)
                grad = weights[0] * cell[:ROWS]
                for j in range(1, TAPS):
                    grad += weights[j] * pltpu.roll(cell, 72 - j, 0)[:ROWS]
                gx_out[g, :, pl.ds(block * WIDTH + part * 128, 128)] = grad.astype(BF16)
                mine = cell[:ROWS]
                sums = [(shifted[j][:ROWS] * mine).sum(0, keepdims=True) for j in range(TAPS)]
                sums.append(mine.sum(0, keepdims=True))
                sums.append(jnp.zeros((3, 128), F32))
                sums_out[g, block, :, inner] = jnp.concatenate(sums, axis=0)

        @pl.when(n < 15)
        def _():
            remote(
                gx_out.at[g],
                left.at[spot, :, pl.ds(0, 2 * WIDTH)],
                gx_send,
                gx_recv.at[spot],
                (dp, 2 * g + x),
            ).start()

        return 0

    lax.fori_loop(0, 16, convolve, 0)
    own_gx = local(gx_out.at[spot], left.at[spot, :, pl.ds(0, 2 * WIDTH)], load_sem.at[0])
    own_gx.start()

    loads[4].wait()
    loads[5].wait()

    def gate_step(n, _):
        for slot in range(2):

            @pl.when(n > 0)
            def _():
                stage_wait(slot)

            up_gradient(2 * n + slot, slot, gate_t, guz_hbm)
        return 0

    lax.fori_loop(0, 2, gate_step, 0)

    def forward(q):
        for copy in weight_copies(q):
            copy.wait_recv()
        for copy in forward_copies(q):
            copy.start()

    forward(0)

    def hand_sums(step, _):
        device = same_x(step)
        remote(
            sums_out.at[(spot + step) % 16], sums_in.at[spot], sums_send, sums_recv, device
        ).start()
        return 0

    sums_pair = remote(pair_out, pair_in, pair_send.at[2], pair_recv.at[2], partner)

    def place(s, first):
        along_z = (1 - s) if first else s
        return along_z * z + (1 - along_z) * y

    def neighbour(s, first, step):
        along_z = (1 - s) if first else s
        far_z = (z + step * along_z) % 4
        far_y = (y + step * (1 - along_z)) % 4
        return (dp, (far_z * 4 + far_y) * 2 + x)

    def term(q, s, step, half):
        target = (place(s, True) + step) % 4
        base = target * (4 - 3 * s)
        stride = 1 + 3 * s
        rows = jnp.concatenate([left[base + stride * j] for j in range(4)], axis=0)
        columns = pl.ds(
            pl.multiple_of(q * CHUNK + s * (CHUNK // 2) + half * TILE, TILE), TILE
        )
        return lax.dot_general(
            rows, right[columns, :], (((1,), (1,)), ((), ())), preferred_element_type=F32
        )

    def hop1(q, s, k):
        step = 1 + 2 * (k % 2)
        return remote(
            send1.at[q, s, k],
            recv1.at[q, s, k],
            s1_send,
            s1_recv.at[q, s, k],
            neighbour(s, True, step),
        )

    def hop2(q, s, k):
        step = 1 + 2 * (k % 2)
        return remote(
            send2.at[q, s, k],
            recv2.at[q, s, k],
            s2_send,
            s2_recv.at[q, s, k],
            neighbour(s, False, step),
        )

    def gx_arrived(dz, dy):
        source = (z + dz) % 4 * 4 + (y + dy) % 4
        block = left.at[source, :, pl.ds(0, 2 * WIDTH)]
        local(block, block, gx_recv.at[source]).wait()

    def first_terms(q):
        for copy in forward_copies(q):
            copy.wait_recv()

        def body(i, _):
            k, s = i // 2, i % 2
            near = k // 2
            step = 2 - near + 2 * near * (k % 2)
            half = (k + near) % 2
            send1[q, s, k] = term(q, s, step, half).astype(BF16)
            hop1(q, s, k).start()
            return 0

        if q > 0:
            lax.fori_loop(0, 8, body, 0)
            return
        for dy in range(4):
            gx_arrived(2, dy)
        lax.fori_loop(0, 2, lambda i, _: body(2 * i, _), 0)
        for dz in (0, 1, 3):
            gx_arrived(dz, 2)
        lax.fori_loop(0, 2, lambda i, _: body(2 * i + 1, _), 0)
        own_gx.wait()
        for dz in (0, 1, 3):
            for dy in (0, 1, 3):
                if dz or dy:
                    gx_arrived(dz, dy)
        gx_pair.start()
        lax.fori_loop(4, 8, body, 0)

    def passed_terms(q):
        def body(i, _):
            half, s = i // 2, i % 2
            value = term(q, s, 1 + 2 * half, half)
            hop1(q, s, half).wait_recv()
            send1[q, s, 4 + half] = (value + recv1[q, s, half].astype(F32)).astype(BF16)
            hop1(q, s, 4 + half).start()
            return 0

        lax.fori_loop(0, 4, body, 0)

    def own_terms(q):
        def body(i, _):
            half, s = i // 2, i % 2
            value = term(q, s, 0, half)
            hop1(q, s, 4 - 2 * half).wait_recv()
            hop1(q, s, 3 + 2 * half).wait_recv()
            value += recv1[q, s, 4 - 2 * half].astype(F32)
            value += recv1[q, s, 3 + 2 * half].astype(F32)
            total[q, s, half] = value.reshape(4, ROWS, TILE)
            return 0

        lax.fori_loop(0, 4, body, 0)

        def spread(i, _):
            k, s = i // 2, i % 2
            near = k // 2
            step = 2 - near + 2 * near * (k % 2)
            half = (k + near) % 2
            send2[q, s, k] = total[q, s, half, (place(s, False) + step) % 4].astype(BF16)
            hop2(q, s, k).start()
            return 0

        lax.fori_loop(0, 8, spread, 0)

    def passed_rows(q):
        def body(i, _):
            half, s = i // 2, i % 2
            value = total[q, s, half, (place(s, False) + 1 + 2 * half) % 4]
            hop2(q, s, half).wait_recv()
            send2[q, s, 4 + half] = (value + recv2[q, s, half].astype(F32)).astype(BF16)
            hop2(q, s, 4 + half).start()
            return 0

        lax.fori_loop(0, 4, body, 0)

    def rows_out(q):
        columns = pl.ds(q * CHUNK, CHUNK)
        return local(out_buf.at[:, columns], out_hbm.at[:, columns], out_sem.at[q])

    def finish(q):
        for s in range(2):
            for half in range(2):
                value = total[q, s, half, place(s, False)]
                hop2(q, s, 4 - 2 * half).wait_recv()
                hop2(q, s, 3 + 2 * half).wait_recv()
                value += recv2[q, s, 4 - 2 * half].astype(F32)
                value += recv2[q, s, 3 + 2 * half].astype(F32)
                out_buf[:, pl.ds(q * CHUNK + s * (CHUNK // 2) + half * TILE, TILE)] = (
                    value.astype(BF16)
                )
        rows_out(q).start()

    def turn_gx(b, _):
        pair = jnp.concatenate([left[b, :, pl.ds(0, WIDTH)], gx_far[b]], axis=0).astype(F32)
        gx_t[:, pl.ds(pl.multiple_of(b * 128, 128), 128)] = pair.T.astype(BF16)
        return 0

    def gx_step(n):
        for slot in range(2):
            stage_wait(slot)
            up_gradient(2 * n + slot, slot, gx_t, gux_hbm)

    loads[6].wait()
    loads[7].wait()
    far_spots = pl.ds(0, 15)
    gx_pair = remote(
        left.at[:, :, pl.ds(WIDTH, WIDTH)], gx_far, pair_send.at[1], pair_recv.at[1], partner
    )
    gate_pair.wait_recv()

    first_terms(0)
    forward(1)
    first_terms(1)
    lax.fori_loop(1, 16, hand_sums, 0)
    sums_in[spot] = sums_out[spot]
    passed_terms(0)
    forward(2)
    forward(3)
    lax.fori_loop(2, 4, gate_step, 0)
    first_terms(2)
    passed_terms(1)
    gx_pair.wait_recv()
    lax.fori_loop(0, 16, turn_gx, 0)
    gx_step(0)
    own_terms(0)
    first_terms(3)
    passed_terms(2)
    gx_step(1)
    own_terms(1)
    passed_rows(0)
    passed_terms(3)
    gx_step(2)
    local(sums_in.at[far_spots], sums_in.at[far_spots], sums_recv).wait()
    small_ref[...] = sums_in[:, 0].sum(0)
    pair_out[...] = sums_in[:, 1].sum(0)
    sums_pair.start()
    own_terms(2)
    passed_rows(1)
    finish(0)
    gx_step(3)
    own_terms(3)
    passed_rows(2)
    finish(1)
    passed_rows(3)
    finish(2)
    finish(3)

    sums_pair.wait_recv()
    small_ref[...] = small_ref[...] + pair_in[...]

    tail.wait_send()
    head.wait_send()
    local(params.at[others], params.at[others], param_send).wait()
    local(sums_out.at[far_spots], sums_out.at[far_spots], sums_send).wait()
    sums_pair.wait_send()
    local(gx_out.at[far_spots], gx_out.at[far_spots], gx_send).wait()
    gate_pair.wait_send()
    gx_pair.wait_send()
    for q in range(CHUNKS):
        for copy in weight_copies(q) + forward_copies(q):
            copy.wait_send()
    for q in range(CHUNKS):
        rows_out(q).wait()
    local(send1, send1, s1_send).wait()
    local(send2, send2, s2_send).wait()
    for slot in range(2):
        stage_wait(slot)


def deliver(
    rows_ref,
    gux_ref,
    guz_ref,
    small_ref,
    rows_out,
    gux_out,
    guz_out,
    taps_out,
    bias_out,
    hold,
    rows_hold,
    small_hold,
    sem,
):
    depth = DIM // PIECES
    steps = [
        (small_ref, small_hold, None),
        (rows_ref, rows_hold, rows_out),
    ]
    for k in range(PIECES):
        part = pl.ds(k * depth, depth)
        steps.append((gux_ref.at[part], hold.at[0, part], gux_out.at[part]))
        steps.append((guz_ref.at[part], hold.at[1, part], guz_out.at[part]))
    reads = [
        pltpu.make_async_copy(src, mid, sem.at[0, k]) for k, (src, mid, _) in enumerate(steps)
    ]
    for copy in reads:
        copy.start()
    writes = []
    for k, (_, mid, dst) in enumerate(steps):
        reads[k].wait()
        if k == 0:
            out = [
                pltpu.make_async_copy(mid.at[pl.ds(0, TAPS)], taps_out, sem.at[1, 0]),
                pltpu.make_async_copy(mid.at[pl.ds(TAPS, 1)], bias_out, sem.at[1, len(steps)]),
            ]
        else:
            out = [pltpu.make_async_copy(mid, dst, sem.at[1, k])]
        for copy in out:
            copy.start()
        writes += out
    for copy in writes:
        copy.wait()


def per_device(grad_act, x_pre, grad_gate, normed_input, conv_weight, conv_bias, up_x, up_z):
    anywhere = pl.BlockSpec(memory_space=pl.ANY)
    vmem = pl.BlockSpec(memory_space=pltpu.VMEM)
    dma = pltpu.SemaphoreType.DMA
    out, gux, guz, small = pl.pallas_call(
        kernel,
        out_shape=(
            jax.ShapeDtypeStruct((ROWS, DIM), BF16),
            jax.ShapeDtypeStruct((DIM, WIDTH), F32),
            jax.ShapeDtypeStruct((DIM, WIDTH), F32),
            jax.ShapeDtypeStruct((8, WIDTH), F32),
        ),
        in_specs=[anywhere] * 8,
        out_specs=(anywhere, anywhere, anywhere, vmem),
        scratch_shapes=[
            pltpu.VMEM((TAPS, WIDTH), F32),
            pltpu.VMEM((1, WIDTH), F32),
            pltpu.VMEM((ROWS, DIM), BF16),
            pltpu.VMEM((ROWS, INNER), BF16),
            pltpu.VMEM((ROWS, INNER), BF16),
            pltpu.VMEM((16, HALF // 2), BF16),
            pltpu.VMEM((16, HALF // 2), BF16),
            pltpu.VMEM((16, HALF), BF16),
            pltpu.VMEM((16, HALF), BF16),
            pltpu.VMEM((GROUP, 8, WIDTH), F32),
            pltpu.VMEM((16, 2, 8, WIDTH), F32),
            pltpu.VMEM((16, 2, 8, WIDTH), F32),
            pltpu.VMEM((8, WIDTH), F32),
            pltpu.VMEM((8, WIDTH), F32),
            pltpu.VMEM((16, ROWS, WIDTH), BF16),
            pltpu.VMEM((WIDTH, TOKENS), BF16),
            pltpu.VMEM((16, ROWS, 2 * WIDTH), BF16),
            pltpu.VMEM((16, ROWS, WIDTH), BF16),
            pltpu.VMEM((WIDTH, TOKENS), BF16),
            pltpu.VMEM((16, ROWS, 4 * WIDTH), BF16),
            pltpu.VMEM((DIM, 4 * WIDTH), BF16),
            pltpu.VMEM((16, 2, ROWS, DIM), BF16),
            pltpu.VMEM((2, 512, WIDTH), F32),
            pltpu.VMEM((CHUNKS, 2, 6, 256, TILE), BF16),
            pltpu.VMEM((CHUNKS, 2, 6, 256, TILE), BF16),
            pltpu.VMEM((CHUNKS, 2, 6, ROWS, TILE), BF16),
            pltpu.VMEM((CHUNKS, 2, 6, ROWS, TILE), BF16),
            pltpu.VMEM((CHUNKS, 2, 2, 4, ROWS, TILE), F32),
            dma((10,)),
            dma((CHUNKS,)),
            dma,
            dma,
            dma((2,)),
            dma((2,)),
            dma,
            dma((16,)),
            dma,
            dma,
            dma((CHUNKS, 2)),
            dma((CHUNKS, 2)),
            dma((CHUNKS, 2)),
            dma((CHUNKS, 2)),
            dma((3,)),
            dma((3,)),
            dma((2,)),
            dma,
            dma((CHUNKS, 2, 6)),
            dma,
            dma((CHUNKS, 2, 6)),
        ],
        compiler_params=pltpu.CompilerParams(
            collective_id=0, has_side_effects=True, vmem_limit_bytes=62 * 1024 * 1024
        ),
        name="conv_up_backward",
    )(
        grad_act,
        x_pre,
        grad_gate.reshape(16, 2, ROWS, WIDTH),
        normed_input.reshape(16, 2, ROWS, DIM),
        conv_weight,
        conv_bias.reshape(1, WIDTH),
        up_x,
        up_z,
    )
    out, gux, guz, taps, bias = pl.pallas_call(
        deliver,
        out_shape=(
            jax.ShapeDtypeStruct((ROWS, DIM), BF16),
            jax.ShapeDtypeStruct((DIM, WIDTH), F32),
            jax.ShapeDtypeStruct((DIM, WIDTH), F32),
            jax.ShapeDtypeStruct((TAPS, WIDTH), F32),
            jax.ShapeDtypeStruct((1, WIDTH), F32),
        ),
        in_specs=[anywhere] * 4,
        out_specs=(anywhere,) * 5,
        scratch_shapes=[
            pltpu.VMEM((2, DIM, WIDTH), F32),
            pltpu.VMEM((ROWS, DIM), BF16),
            pltpu.VMEM((8, WIDTH), F32),
            dma((2, 2 * PIECES + 3)),
        ],
        compiler_params=pltpu.CompilerParams(vmem_limit_bytes=62 * 1024 * 1024),
        name="deliver",
    )(out, gux, guz, small)
    return out, gux, guz, taps, bias.reshape(WIDTH)


def solution(mesh):
    placed = (
        P(("dp", "tensor"), None),
        P(("dp", "tensor"), None),
        P("dp", "tensor"),
        P("dp", None),
        P(None, "tensor"),
        P("tensor"),
        P(None, "tensor"),
        P(None, "tensor"),
    )
    return jax.shard_map(
        per_device,
        mesh=mesh,
        in_specs=placed,
        out_specs=(
            P(("dp", "tensor"), None),
            P("dp", "tensor"),
            P("dp", "tensor"),
            P("dp", "tensor"),
            P(("dp", "tensor")),
        ),
        check_vma=False,
    )
```
